32 devices in a mesh: leaf: 8 (over y, x, core), col: 4 (over z).
Axes of the slice: x: 2, y: 2, z: 4, core: 2. Of those that a mesh axis runs over, the one named last changes fastest.
Arguments:
- histograms: bfloat16 [4, 32, 1024, 512], P(None, 'leaf', 'col'), may hold values from -6 to 6
- diag_inv: bfloat16 [4, 32, 512, 512], P(None, 'leaf', 'col'), as said below
- below_panel: bfloat16 [4, 32, 256, 512], P(None, 'leaf', 'col'), may hold values from -0.1875 to 0.1875
- parent_map: int32 [3, 32], P(None, 'leaf'), may hold values from 0 to 31, as said below
- row_lists: int32 [3, 32, 256], P(None, 'leaf'), may hold values from 0 to 511, as said below
Outputs:
- solution: bfloat16 [4, 32, 1024, 512], P(None, 'leaf', 'col')
- upward: bfloat16 [32, 1024, 256], P('leaf', 'col')
The draws below stay inside these ranges and needn't reach their ends.
Inputs may be any that keep to these rules, and one draw needn't show every extreme that they name: `parent_map`: entry [l, j] names a supernode of tier l + 1 whose owner (index // 4) is the owner of supernode j (j // 4) or the leaf index that differs from it in bit l mod log2(8); at every tier some leaf index sends all its updates to that other index. `row_lists`: the 256 entries of each list are distinct. `diag_inv`: every block is lower triangular with a positive diagonal.
All inputs are finite; a program needn't handle non-finite values.
Results may differ from the reference program's by a relative error of at most 0.012.
Values may be sent and summed in bfloat16 or wider, within the bound.
No kernel may reach another device: no remote copies, remote signals or barrier semaphores. Data moves between devices by JAX's collectives and lax.ppermute only.
A program may use at most 64 MiB of HBM per device.

```python
import math
import jax
import jax.numpy as jnp
from jax import lax

W = 512
R = 256
COLS = 1024
LEVELS = 4
SN_DEV = 4
NS = 32
N_LEAF = 8


def draw_diag_inv(key, part):
    key_lower, key_pivot = jax.random.split(key)
    below_diag = jax.random.normal(key_lower, (LEVELS, NS, W, W), jnp.float32) * (0.8 / math.sqrt(W))
    pivots = jax.random.uniform(key_pivot, (LEVELS, NS, W), jnp.float32, 0.6, 1.2)
    positions = jnp.arange(W)
    strictly = (positions[:, None] > positions[None, :]).astype(jnp.float32)
    identity = (positions[:, None] == positions[None, :]).astype(jnp.float32)
    return (below_diag * strictly + pivots[..., None] * identity).astype(jnp.bfloat16)


def draw_parent_map(key, part):
    key_tend, key_roll, key_force, key_slot = jax.random.split(key, 4)
    bit_count = max(N_LEAF.bit_length() - 1, 1)
    children = jnp.arange(NS, dtype=jnp.int32)
    owners = children // SN_DEV
    tiers = jnp.arange(LEVELS - 1, dtype=jnp.int32)
    tendency = jax.random.randint(key_tend, (LEVELS - 1, N_LEAF), 0, 5)
    rolled = jax.random.randint(key_roll, (LEVELS - 1, NS), 0, 4)
    leaving = rolled < tendency[:, owners]
    forced = jax.random.randint(key_force, (LEVELS - 1, 1), 0, N_LEAF)
    leaving = jnp.logical_or(leaving, owners[None, :] == forced)
    partner_bit = jnp.left_shift(jnp.ones_like(tiers), tiers % bit_count)[:, None]
    partner = jnp.bitwise_xor(owners[None, :], partner_bit)
    target = jnp.where(leaving, partner, owners[None, :])
    slots = jax.random.randint(key_slot, (LEVELS - 1, NS), 0, SN_DEV)
    return (target * SN_DEV + slots).astype(jnp.int32)


def draw_row_lists(key, part):
    key_list = jax.random.split(key, (LEVELS - 1) * NS)
    orders = jax.vmap(lambda single: jax.random.permutation(single, W)[:R])(key_list)
    return orders.reshape(LEVELS - 1, NS, R).astype(jnp.int32)


def steps_of(key, shape, shards, smallest, high):
    level = 1.0
    for position, blocks in shards:
        draws = jax.random.uniform(jax.random.fold_in(jax.random.fold_in(key, 6), position), (blocks,), jnp.float32, smallest / len(shards), high / len(shards))
        level = level * jnp.repeat(jnp.exp(draws), shape[position] // blocks).reshape((-1,) + (1,) * (len(shape) - 1 - position))
    return level


def bell_draw(rng, dims, spread, limit, cuts=(), kind=jnp.bfloat16):
    entries = jax.random.normal(rng, dims, jnp.float32) * spread
    if len(cuts) > 0:
        entries = steps_of(rng, dims, cuts, -0.22, 0.18) * entries
    return jnp.clip(entries, min=-limit, max=limit).astype(kind)


def setup_inputs(seed: int = 0) -> dict:
    seeds = jax.random.split(jax.random.key(seed), 6)
    histograms = bell_draw(seeds[0], (LEVELS, NS, COLS, W), 1.0, 6.0, ((1, 8), (2, 4)))
    diag_inv = draw_diag_inv(jax.random.fold_in(seeds[5], 71), 0)
    below_panel = bell_draw(seeds[2], (LEVELS, NS, R, W), (2 * W) ** -0.5, 0.1875, ((1, 8), (2, 4)))
    parent_map = draw_parent_map(jax.random.fold_in(seeds[5], 71), 0)
    row_lists = draw_row_lists(jax.random.fold_in(seeds[5], 71), 0)
    return {"histograms": histograms, "diag_inv": diag_inv, "below_panel": below_panel, "parent_map": parent_map, "row_lists": row_lists}


def reference(histograms, diag_inv, below_panel, parent_map, row_lists):
    incoming = jnp.zeros((NS, COLS, W), jnp.float32)
    columns = jnp.arange(COLS, dtype=jnp.int32)
    solved = []
    upward = jnp.zeros((NS, COLS, R), jnp.bfloat16)
    for height in range(LEVELS):
        source = (histograms[height].astype(jnp.float32) - incoming).astype(jnp.bfloat16)
        source = lax.optimization_barrier(source)
        result = jnp.einsum("scw,svw->scv", source.astype(jnp.float32), diag_inv[height].astype(jnp.float32))
        answer = result.astype(jnp.bfloat16)
        answer = lax.optimization_barrier(answer)
        solved.append(answer)
        update = jnp.einsum("scw,srw->scr", answer.astype(jnp.float32), below_panel[height].astype(jnp.float32))
        if height == LEVELS - 1:
            upward = update.astype(jnp.bfloat16)
        else:
            targets = parent_map[height].astype(jnp.int32)
            lists = row_lists[height].astype(jnp.int32)
            incoming = jnp.zeros((NS, COLS, W), jnp.float32).at[targets[:, None, None], columns[None, :, None], lists[:, None, :]].add(update)
    return jnp.stack(solved), upward
```

```python
import functools

import jax
import jax.numpy as jnp
from jax import lax
from jax.experimental import pallas as pl
from jax.experimental.pallas import tpu as pltpu
from jax.sharding import PartitionSpec as P

LANES = 128
SPARE = 16
ANY = pl.BlockSpec(memory_space=pl.ANY)
SMEM = pl.BlockSpec(memory_space=pltpu.SMEM)


def swap_route(axis, apart):
    count = lax.axis_size(axis)
    pairs = []
    for low in range(count):
        high = low | 1 << apart
        if high != low and high < count:
            pairs += [(low, high), (high, low)]
    return pairs


def dot_rows(left, right):
    return lax.dot_general(
        left, right, (((1,), (1,)), ((), ())), preferred_element_type=jnp.float32
    )


def spread_rows(update, lists, slots, per_device, node_width):
    slot_match = (
        slots[:, None, None, None] == jnp.arange(per_device, dtype=jnp.int32)[None, None, :, None]
    )
    row_match = (
        lists[:, :, None, None] == jnp.arange(node_width, dtype=jnp.int32)[None, None, None, :]
    )
    placing = jnp.logical_and(slot_match, row_match).astype(jnp.bfloat16)
    return jnp.einsum(
        "scr,srpw->pcw", update.astype(jnp.bfloat16), placing, preferred_element_type=jnp.float32
    )


def gathered_plan(histograms, diag_inv, below_panel, parent_map, row_lists):
    tier_count, per_device, _, node_width = histograms.shape
    bit_count = max(lax.axis_size("leaf").bit_length() - 1, 1)
    myself = lax.axis_index("leaf")
    incoming = jnp.zeros(histograms.shape[1:], jnp.float32)
    solved = []
    for height in range(tier_count):
        source = (histograms[height].astype(jnp.float32) - incoming).astype(jnp.bfloat16)
        diag = lax.all_gather(diag_inv[height], "col", axis=1, tiled=True)
        below = lax.all_gather(below_panel[height], "col", axis=1, tiled=True)
        answer = jnp.einsum(
            "scw,svw->scv", source, diag, preferred_element_type=jnp.float32
        ).astype(jnp.bfloat16)
        solved.append(answer)
        update = jnp.einsum("scw,srw->scr", answer, below, preferred_element_type=jnp.float32)
        if height == tier_count - 1:
            break
        owners = parent_map[height] // per_device
        slots = parent_map[height] % per_device
        staying = owners == myself
        lists = row_lists[height]
        kept = spread_rows(update, lists, jnp.where(staying, slots, -1), per_device, node_width)
        leaving = spread_rows(update, lists, jnp.where(staying, -1, slots), per_device, node_width)
        path = swap_route("leaf", height % bit_count)
        arrived = lax.ppermute(leaving.astype(jnp.bfloat16), "leaf", path)
        incoming = kept + arrived.astype(jnp.float32)
    return jnp.stack(solved), update.astype(jnp.bfloat16)


def layout(per_device, below_rows, node_width):
    block = per_device * LANES
    tri = block // 2
    below = per_device * below_rows * (node_width // LANES)
    return block, tri, below, block + tri + SPARE + below


def pack_kernel(place_ref, diag_ref, below_ref, base_ref, rest_ref):
    per_device, below_rows, node_width = below_ref.shape[1:]
    block, tri, _, total = layout(per_device, below_rows, node_width)
    for s in range(per_device):
        rows = slice(s * LANES, (s + 1) * LANES)
        base_ref[rows, :] = diag_ref[0, s, :, :LANES]
        for k in range(3):
            rest_ref[k * block + s * LANES : k * block + (s + 1) * LANES, :] = diag_ref[
                0, s, :, k * LANES : (k + 1) * LANES
            ]
        start = block + tri + SPARE + s * below_rows * (node_width // LANES)
        for k in range(node_width // LANES):
            base_ref[start + k * below_rows : start + (k + 1) * below_rows, :] = below_ref[
                0, s, :, k * LANES : (k + 1) * LANES
            ]
    rest_ref[3 * block :, :] = jnp.zeros((total - 3 * block, LANES), rest_ref.dtype)
    down = lax.broadcasted_iota(jnp.int32, (LANES, LANES), 0)
    across = lax.broadcasted_iota(jnp.int32, (LANES, LANES), 1)
    for place in range(4):

        @pl.when(place_ref[0] == place)
        def _():
            columns = slice(place * LANES, (place + 1) * LANES)
            pivots = []
            for pair in range(per_device // 2):
                first = diag_ref[0, 2 * pair, :, columns].astype(jnp.float32)
                second = diag_ref[0, 2 * pair + 1, :, columns].astype(jnp.float32)
                both = jnp.where(down >= across, first, second.T)
                base_ref[block + pair * LANES : block + (pair + 1) * LANES, :] = both.astype(
                    base_ref.dtype
                )
                pivots.append(
                    jnp.sum(jnp.where(down == across, second, 0.0), axis=0, keepdims=True)
                )
            pivots.append(jnp.zeros((SPARE - len(pivots), LANES), jnp.float32))
            base_ref[block + tri : block + tri + SPARE, :] = jnp.concatenate(pivots, 0).astype(
                base_ref.dtype
            )


def pack(place, diag_inv, below_panel, height):
    _, per_device, rows, node_width = diag_inv.shape
    below_rows = below_panel.shape[2]
    total = layout(per_device, below_rows, node_width)[-1]
    shape = jax.ShapeDtypeStruct((total, LANES), diag_inv.dtype)
    return pl.pallas_call(
        pack_kernel,
        grid=(1,),
        in_specs=[
            SMEM,
            pl.BlockSpec((1, per_device, rows, node_width), lambda i: (height, 0, 0, 0)),
            pl.BlockSpec((1, per_device, below_rows, node_width), lambda i: (height, 0, 0, 0)),
        ],
        out_specs=[pl.BlockSpec((total, LANES), lambda i: (0, 0))] * 2,
        out_shape=[shape, shape],
        cost_estimate=pl.CostEstimate(
            flops=0, bytes_accessed=4 * total * LANES * 2, transcendentals=0
        ),
        name=f"pack_{height}",
    )(place, diag_inv, below_panel)


def source_kernel(slots_ref, hist_ref, own_ref, peer_ref, own_lists, peer_lists, out_ref, total):
    per_device, below = own_ref.shape[0], own_ref.shape[2]
    width = out_ref.shape[2]
    total[...] = hist_ref[0].astype(jnp.float32)
    target = lax.broadcasted_iota(jnp.int32, (width, below), 0)
    for refs in ((own_ref, own_lists, 0), (peer_ref, peer_lists, per_device)):
        update_ref, lists_ref, offset = refs
        for s in range(per_device):
            slot = slots_ref[offset + s]

            @pl.when(slot >= 0)
            def _():
                here = target == lists_ref[s : s + 1, :]
                placing = jnp.where(here, 1.0, 0.0).astype(jnp.bfloat16)
                total[slot] = total[slot] - dot_rows(update_ref[s], placing)

    out_ref[...] = total[...].astype(out_ref.dtype)


def source_of(histograms, height, own, peer, slots, own_lists, peer_lists):
    _, per_device, columns, width = histograms.shape
    below = own.shape[2]
    whole = pl.BlockSpec((per_device, columns, below), lambda i: (0, 0, 0))
    lists = pl.BlockSpec((per_device, below), lambda i: (0, 0))
    return pl.pallas_call(
        source_kernel,
        grid=(1,),
        in_specs=[
            SMEM,
            pl.BlockSpec((1, per_device, columns, width), lambda i: (height, 0, 0, 0)),
            whole,
            whole,
            lists,
            lists,
        ],
        out_specs=pl.BlockSpec((per_device, columns, width), lambda i: (0, 0, 0)),
        out_shape=jax.ShapeDtypeStruct((per_device, columns, width), jnp.bfloat16),
        scratch_shapes=[pltpu.VMEM((per_device, columns, width), jnp.float32)],
        compiler_params=pltpu.CompilerParams(vmem_limit_bytes=32 << 20),
        cost_estimate=pl.CostEstimate(
            flops=4 * per_device * columns * width * below,
            bytes_accessed=6 * per_device * columns * width,
            transcendentals=0,
        ),
        name=f"source_{height}",
    )(slots, histograms, own, peer, own_lists, peer_lists)


def solve_kernel(
    group_at,
    has_prior,
    place_ref,
    source_ref,
    base,
    rest,
    left0,
    left1,
    left2,
    left3,
    right0,
    right1,
    right2,
    *refs,
):
    if has_prior:
        refs = refs[1:]
    solved_ref, update_ref, tail, off, diag, below, sems = refs
    below_width = below.shape[1]
    below_rows = below.shape[0] // 4
    block = off.shape[0] // 6
    tri = block // 2
    step = pl.program_id(0)

    @pl.when(step == 0)
    def _():
        def head(ref):
            return ref.at[pl.ds(0, block)]

        def foot(ref):
            return ref.at[pl.ds(block, tail.shape[1])]

        def all_off(ref):
            return ref.at[pl.ds(0, 3 * block)]

        r0, r1, r2 = (r.at[group_at] for r in (right0, right1, right2))
        second = rest.at[pl.ds(block, block)]
        where = (
            (foot(base), foot(left0), foot(left1), foot(left2),
             head(left0), head(left1), head(left2), all_off(left3)),
            (foot(r0), foot(base), foot(left0), foot(left1),
             head(base), head(left0), head(left1), all_off(left2)),
            (foot(r1), foot(r0), foot(base), foot(left0),
             head(r0), head(base), second, all_off(left1)),
            (foot(r2), foot(r1), foot(r0), foot(base),
             head(r1), head(r0), head(r2), all_off(rest)),
        )
        into = [tail.at[j] for j in range(4)]
        into += [off.at[pl.ds(k * block, block)] for k in range(3)]
        into += [off.at[pl.ds(3 * block, 3 * block)]]
        for place in range(4):

            @pl.when(place_ref[0] == place)
            def _():
                copies = [
                    pltpu.make_async_copy(src, dst, sems.at[i])
                    for i, (src, dst) in enumerate(zip(where[place], into))
                ]
                for copy in copies:
                    copy.start()
                for copy in copies:
                    copy.wait()

    down = lax.broadcasted_iota(jnp.int32, (LANES, LANES), 0)
    across = lax.broadcasted_iota(jnp.int32, (LANES, LANES), 1)
    zero = jnp.zeros((LANES, LANES), diag.dtype)
    per_step = solved_ref.shape[1]
    for part in range(per_step):
        s = step * per_step + part
        row = pl.multiple_of(s * LANES, LANES)
        spot = 0
        for j in range(4):
            rows = slice(j * LANES, (j + 1) * LANES)
            for k in range(j):
                diag[part, rows, k * LANES : (k + 1) * LANES] = off[
                    pl.ds(pl.multiple_of(spot * block + row, LANES), LANES), :
                ]
                spot += 1
            pair = pl.multiple_of(step * LANES, LANES)
            both = tail[j, pl.ds(pair, LANES), :].astype(jnp.float32)
            if part == 0:
                mine = jnp.where(down >= across, both, 0.0)
            else:
                pivots = tail[j, tri : tri + SPARE, :].astype(jnp.float32)
                which = lax.broadcasted_iota(jnp.int32, (SPARE, LANES), 0) == step
                pivot = jnp.sum(jnp.where(which, pivots, 0.0), axis=0, keepdims=True)
                mine = jnp.where(
                    down > across, both.T, jnp.where(down == across, pivot, 0.0)
                )
            diag[part, rows, rows] = mine.astype(diag.dtype)
            if j % 2 == 0:
                diag[part, rows, (j + 1) * LANES : (j + 2) * LANES] = zero
            first = tri + SPARE + s * below_rows * (below_width // LANES)
            for k in range(below_width // LANES):
                below[j * below_rows : (j + 1) * below_rows, k * LANES : (k + 1) * LANES] = tail[
                    j, pl.ds(pl.multiple_of(first + k * below_rows, 16), below_rows), :
                ]
        half = 2 * LANES
        x = source_ref[part]
        solved_ref[0, part, :, :half] = dot_rows(
            x[:, :half], diag[part, :half, :half]
        ).astype(solved_ref.dtype)
        solved_ref[0, part, :, half:] = dot_rows(x, diag[part, half:, :]).astype(solved_ref.dtype)
        update_ref[part] = dot_rows(solved_ref[0, part], below[...]).astype(update_ref.dtype)


def solve(place, source, first_block, height, sizes, own, lefts, rights, group_at, prior):
    tiers, per_device, below_rows = sizes
    _, columns, width = source.shape
    below = 4 * below_rows
    block, _, _, total = layout(per_device, below_rows, width)
    has_prior = prior is not None
    operands = [place, source, *own, *lefts, *rights] + ([prior] if has_prior else [])
    return pl.pallas_call(
        functools.partial(solve_kernel, group_at, has_prior),
        grid=(per_device // 2,),
        in_specs=[SMEM, pl.BlockSpec((2, columns, width), lambda i: (first_block + i, 0, 0))]
        + [ANY] * (len(operands) - 2),
        out_specs=[
            pl.BlockSpec((1, 2, columns, width), lambda i: (height, i, 0, 0)),
            pl.BlockSpec((2, columns, below), lambda i: (i, 0, 0)),
        ],
        out_shape=[
            jax.ShapeDtypeStruct((tiers, per_device, columns, width), jnp.bfloat16),
            jax.ShapeDtypeStruct((per_device, columns, below), jnp.bfloat16),
        ],
        scratch_shapes=[
            pltpu.VMEM((4, total - block, LANES), jnp.bfloat16),
            pltpu.VMEM((6 * block, LANES), jnp.bfloat16),
            pltpu.VMEM((2, width, width), jnp.bfloat16),
            pltpu.VMEM((below, width), jnp.bfloat16),
            pltpu.SemaphoreType.DMA((8,)),
        ],
        input_output_aliases={len(operands) - 1: 0} if has_prior else {},
        compiler_params=pltpu.CompilerParams(vmem_limit_bytes=32 << 20),
        cost_estimate=pl.CostEstimate(
            flops=2 * per_device * columns * width * (width + below),
            bytes_accessed=6 * per_device * columns * width,
            transcendentals=0,
        ),
        name=f"solve_{height}",
    )(*operands)


def after(value, *earlier):
    return lax.optimization_barrier((value, *(e.reshape(-1, LANES)[:8] for e in earlier)))[0]


def send(value, route):
    return lax.ppermute(value, "col", route)


def line_plan(histograms, diag_inv, below_panel, parent_map, row_lists):
    tiers, per_device, columns, width = histograms.shape
    below_rows = below_panel.shape[2]
    block, _, _, total = layout(per_device, below_rows, width)
    place = lax.axis_index("col").astype(jnp.int32)
    place_ref = place[None]
    up = [(0, 1), (1, 2), (2, 3)]
    down = [(1, 0), (2, 1), (3, 2)]
    packs = [pack(place_ref, diag_inv, below_panel, t) for t in range(tiers)]

    lefts = []
    for base, rest in packs:
        left0 = send(base, down)
        mixed = jnp.concatenate([rest[block : 2 * block], left0[block:]], 0)
        left1 = send(jnp.where(place == 1, left0, jnp.where(place == 2, mixed, rest)), down)
        left2 = send(left1, down[:2])
        left3 = send(left2[: 3 * block], down[:1])
        lefts.append((left0, left1, left2, left3))

    rights = []
    for group in right_groups(tiers):
        bases = jnp.stack([packs[t][0] for t in group])
        if group[0] > 0:
            bases = after(bases, lefts[0][1])
        right0 = send(bases, up)
        right1 = send(right0, up[1:])
        second = jnp.stack([packs[t][1][block : 2 * block] for t in group])
        right2 = send(jnp.concatenate([second, right1[:, block:]], 1), up[2:])
        rights += [((right0, right1, right2), i) for i in range(len(group))]

    myself = lax.axis_index("leaf")
    count = lax.axis_size("leaf")
    bit_count = max(count.bit_length() - 1, 1)
    table = jnp.concatenate([parent_map[:, :, None], row_lists], 2)
    tables = lax.all_gather(table, "leaf")
    source, first_block = histograms.reshape(-1, columns, width), 0
    solved = None
    for t in range(tiers):
        right, group_at = rights[t]
        solved, update = solve(
            place_ref,
            source,
            first_block,
            t,
            (tiers, per_device, below_rows),
            packs[t],
            lefts[t],
            right,
            group_at,
            solved,
        )
        if t == tiers - 1:
            break
        bit = t % bit_count
        peer = lax.ppermute(update, "leaf", swap_route("leaf", bit))
        partner = jnp.bitwise_xor(myself, 1 << bit)
        theirs = lax.dynamic_index_in_dim(tables, jnp.minimum(partner, count - 1), 0, False)[t]
        parents = jnp.concatenate([parent_map[t], theirs[:, 0]])
        exists = jnp.repeat(jnp.stack([partner >= 0, partner < count]), per_device)
        mine = jnp.logical_and(parents // per_device == myself, exists)
        slots = jnp.where(mine, parents % per_device, -1)
        source = source_of(histograms, t + 1, update, peer, slots, row_lists[t], theirs[:, 1:])
        first_block = 0
    return solved, update


def right_groups(tiers):
    return [[0], list(range(1, tiers))]


def on_device(histograms, diag_inv, below_panel, parent_map, row_lists):
    _, per_device, rows, width = diag_inv.shape
    fits = (
        lax.axis_size("col") == 4
        and rows == LANES
        and width == 4 * rows
        and per_device % 2 == 0
        and per_device <= 2 * SPARE
        and below_panel.shape[2] % 16 == 0
        and histograms.shape[2] % 16 == 0
        and histograms.shape[0] > 1
    )
    plan = line_plan if fits else gathered_plan
    return plan(histograms, diag_inv, below_panel, parent_map, row_lists)


def solution(mesh):
    return jax.shard_map(
        on_device,
        mesh=mesh,
        in_specs=(
            P(None, "leaf", "col", None),
            P(None, "leaf", "col", None),
            P(None, "leaf", "col", None),
            P(None, "leaf"),
            P(None, "leaf", None),
        ),
        out_specs=(P(None, "leaf", "col", None), P("leaf", "col", None)),
        check_vma=False,
    )
```

```python
import functools

import jax
import jax.numpy as jnp
from jax import lax
from jax.experimental import pallas as pl
from jax.experimental.pallas import tpu as pltpu
from jax.sharding import PartitionSpec as P

PLAN = "LR"
TIE = 0
TIE_TO = (1,)
TABLE_TIE = True
RIGHT_GROUPS = [[0], [1], [2], [3]]
LANES = 128
SPARE = 16
ANY = pl.BlockSpec(memory_space=pl.ANY)
SMEM = pl.BlockSpec(memory_space=pltpu.SMEM)


def swap_route(axis, apart):
    count = lax.axis_size(axis)
    pairs = []
    for low in range(count):
        high = low | 1 << apart
        if high != low and high < count:
            pairs += [(low, high), (high, low)]
    return pairs


def dot_rows(left, right):
    return lax.dot_general(
        left, right, (((1,), (1,)), ((), ())), preferred_element_type=jnp.float32
    )


def spread_rows(update, lists, slots, per_device, node_width):
    slot_match = (
        slots[:, None, None, None] == jnp.arange(per_device, dtype=jnp.int32)[None, None, :, None]
    )
    row_match = (
        lists[:, :, None, None] == jnp.arange(node_width, dtype=jnp.int32)[None, None, None, :]
    )
    placing = jnp.logical_and(slot_match, row_match).astype(jnp.bfloat16)
    return jnp.einsum(
        "scr,srpw->pcw", update.astype(jnp.bfloat16), placing, preferred_element_type=jnp.float32
    )


def gathered_plan(histograms, diag_inv, below_panel, parent_map, row_lists):
    tier_count, per_device, _, node_width = histograms.shape
    bit_count = max(lax.axis_size("leaf").bit_length() - 1, 1)
    myself = lax.axis_index("leaf")
    incoming = jnp.zeros(histograms.shape[1:], jnp.float32)
    solved = []
    for height in range(tier_count):
        source = (histograms[height].astype(jnp.float32) - incoming).astype(jnp.bfloat16)
        diag = lax.all_gather(diag_inv[height], "col", axis=1, tiled=True)
        below = lax.all_gather(below_panel[height], "col", axis=1, tiled=True)
        answer = jnp.einsum(
            "scw,svw->scv", source, diag, preferred_element_type=jnp.float32
        ).astype(jnp.bfloat16)
        solved.append(answer)
        update = jnp.einsum("scw,srw->scr", answer, below, preferred_element_type=jnp.float32)
        if height == tier_count - 1:
            break
        owners = parent_map[height] // per_device
        slots = parent_map[height] % per_device
        staying = owners == myself
        lists = row_lists[height]
        kept = spread_rows(update, lists, jnp.where(staying, slots, -1), per_device, node_width)
        leaving = spread_rows(update, lists, jnp.where(staying, -1, slots), per_device, node_width)
        path = swap_route("leaf", height % bit_count)
        arrived = lax.ppermute(leaving.astype(jnp.bfloat16), "leaf", path)
        incoming = kept + arrived.astype(jnp.float32)
    return jnp.stack(solved), update.astype(jnp.bfloat16)


def layout(per_device, below_rows, node_width):
    block = per_device * LANES
    tri = block // 2
    below = per_device * below_rows * (node_width // LANES)
    return block, tri, below, block + tri + SPARE + below


def pack_kernel(place_ref, diag_ref, below_ref, base_ref, rest_ref):
    per_device, below_rows, node_width = below_ref.shape[1:]
    block, tri, _, total = layout(per_device, below_rows, node_width)
    for s in range(per_device):
        rows = slice(s * LANES, (s + 1) * LANES)
        base_ref[rows, :] = diag_ref[0, s, :, :LANES]
        for k in range(3):
            rest_ref[k * block + s * LANES : k * block + (s + 1) * LANES, :] = diag_ref[
                0, s, :, k * LANES : (k + 1) * LANES
            ]
        start = block + tri + SPARE + s * below_rows * (node_width // LANES)
        for k in range(node_width // LANES):
            base_ref[start + k * below_rows : start + (k + 1) * below_rows, :] = below_ref[
                0, s, :, k * LANES : (k + 1) * LANES
            ]
    rest_ref[3 * block :, :] = jnp.zeros((total - 3 * block, LANES), rest_ref.dtype)
    down = lax.broadcasted_iota(jnp.int32, (LANES, LANES), 0)
    across = lax.broadcasted_iota(jnp.int32, (LANES, LANES), 1)
    for place in range(4):

        @pl.when(place_ref[0] == place)
        def _():
            columns = slice(place * LANES, (place + 1) * LANES)
            pivots = []
            for pair in range(per_device // 2):
                first = diag_ref[0, 2 * pair, :, columns].astype(jnp.float32)
                second = diag_ref[0, 2 * pair + 1, :, columns].astype(jnp.float32)
                both = jnp.where(down >= across, first, second.T)
                base_ref[block + pair * LANES : block + (pair + 1) * LANES, :] = both.astype(
                    base_ref.dtype
                )
                pivots.append(
                    jnp.sum(jnp.where(down == across, second, 0.0), axis=0, keepdims=True)
                )
            pivots.append(jnp.zeros((SPARE - len(pivots), LANES), jnp.float32))
            base_ref[block + tri : block + tri + SPARE, :] = jnp.concatenate(pivots, 0).astype(
                base_ref.dtype
            )


def pack(place, diag_inv, below_panel, height):
    _, per_device, rows, node_width = diag_inv.shape
    below_rows = below_panel.shape[2]
    total = layout(per_device, below_rows, node_width)[-1]
    shape = jax.ShapeDtypeStruct((total, LANES), diag_inv.dtype)
    return pl.pallas_call(
        pack_kernel,
        grid=(1,),
        in_specs=[
            SMEM,
            pl.BlockSpec((1, per_device, rows, node_width), lambda i: (height, 0, 0, 0)),
            pl.BlockSpec((1, per_device, below_rows, node_width), lambda i: (height, 0, 0, 0)),
        ],
        out_specs=[pl.BlockSpec((total, LANES), lambda i: (0, 0))] * 2,
        out_shape=[shape, shape],
        cost_estimate=pl.CostEstimate(
            flops=0, bytes_accessed=4 * total * LANES * 2, transcendentals=0
        ),
        name=f"pack_{height}",
    )(place, diag_inv, below_panel)


def source_kernel(slots_ref, hist_ref, own_ref, peer_ref, own_lists, peer_lists, out_ref, total):
    per_device, below = own_ref.shape[0], own_ref.shape[2]
    width = out_ref.shape[2]
    total[...] = hist_ref[0].astype(jnp.float32)
    target = lax.broadcasted_iota(jnp.int32, (width, below), 0)
    for refs in ((own_ref, own_lists, 0), (peer_ref, peer_lists, per_device)):
        update_ref, lists_ref, offset = refs
        for s in range(per_device):
            slot = slots_ref[offset + s]

            @pl.when(slot >= 0)
            def _():
                here = target == lists_ref[s : s + 1, :]
                placing = jnp.where(here, 1.0, 0.0).astype(jnp.bfloat16)
                total[slot] = total[slot] - dot_rows(update_ref[s], placing)

    out_ref[...] = total[...].astype(out_ref.dtype)


def source_of(histograms, height, own, peer, slots, own_lists, peer_lists):
    _, per_device, columns, width = histograms.shape
    below = own.shape[2]
    whole = pl.BlockSpec((per_device, columns, below), lambda i: (0, 0, 0))
    lists = pl.BlockSpec((per_device, below), lambda i: (0, 0))
    return pl.pallas_call(
        source_kernel,
        grid=(1,),
        in_specs=[
            SMEM,
            pl.BlockSpec((1, per_device, columns, width), lambda i: (height, 0, 0, 0)),
            whole,
            whole,
            lists,
            lists,
        ],
        out_specs=pl.BlockSpec((per_device, columns, width), lambda i: (0, 0, 0)),
        out_shape=jax.ShapeDtypeStruct((per_device, columns, width), jnp.bfloat16),
        scratch_shapes=[pltpu.VMEM((per_device, columns, width), jnp.float32)],
        compiler_params=pltpu.CompilerParams(vmem_limit_bytes=32 << 20),
        cost_estimate=pl.CostEstimate(
            flops=4 * per_device * columns * width * below,
            bytes_accessed=6 * per_device * columns * width,
            transcendentals=0,
        ),
        name=f"source_{height}",
    )(slots, histograms, own, peer, own_lists, peer_lists)


def solve_kernel(
    group_at,
    has_prior,
    place_ref,
    source_ref,
    base,
    rest,
    left0,
    left1,
    left2,
    left3,
    right0,
    right1,
    right2,
    *refs,
):
    if has_prior:
        refs = refs[1:]
    solved_ref, update_ref, tail, off, diag, below, sems = refs
    below_width = below.shape[1]
    below_rows = below.shape[0] // 4
    block = off.shape[0] // 6
    tri = block // 2
    step = pl.program_id(0)

    @pl.when(step == 0)
    def _():
        def head(ref):
            return ref.at[pl.ds(0, block)]

        def foot(ref):
            return ref.at[pl.ds(block, tail.shape[1])]

        def all_off(ref):
            return ref.at[pl.ds(0, 3 * block)]

        r0, r1, r2 = (r if PLAN == "SM" else r.at[group_at] for r in (right0, right1, right2))
        second = rest.at[pl.ds(block, block)]
        if PLAN == "SM":
            s0, s1, s2, s3, m0, m1, m2 = left0, left1, left2, left3, right0, right1, right2
            where = (
                (foot(base), foot(s0), foot(s1), foot(s2),
                 head(s0), head(s1), head(s2), all_off(s3)),
                (foot(s0), foot(base), foot(m0), foot(m1),
                 head(base), head(m0), head(m1), all_off(m2)),
                (foot(m1), foot(m0), foot(base), foot(s0),
                 head(m0), head(base), second, all_off(s1)),
                (foot(s2), foot(s1), foot(s0), foot(base),
                 head(s1), head(s0), head(s2), all_off(rest)),
            )
        else:
          where = (
            (foot(base), foot(left0), foot(left1), foot(left2),
             head(left0), head(left1), head(left2), all_off(left3)),
            (foot(r0), foot(base), foot(left0), foot(left1),
             head(base), head(left0), head(left1), all_off(left2)),
            (foot(r1), foot(r0), foot(base), foot(left0),
             head(r0), head(base), second, all_off(left1)),
            (foot(r2), foot(r1), foot(r0), foot(base),
             head(r1), head(r0), head(r2), all_off(rest)),
        )
        into = [tail.at[j] for j in range(4)]
        into += [off.at[pl.ds(k * block, block)] for k in range(3)]
        into += [off.at[pl.ds(3 * block, 3 * block)]]
        for place in range(4):

            @pl.when(place_ref[0] == place)
            def _():
                copies = [
                    pltpu.make_async_copy(src, dst, sems.at[i])
                    for i, (src, dst) in enumerate(zip(where[place], into))
                ]
                for copy in copies:
                    copy.start()
                for copy in copies:
                    copy.wait()

    down = lax.broadcasted_iota(jnp.int32, (LANES, LANES), 0)
    across = lax.broadcasted_iota(jnp.int32, (LANES, LANES), 1)
    zero = jnp.zeros((LANES, LANES), diag.dtype)
    per_step = solved_ref.shape[1]
    for part in range(per_step):
        s = step * per_step + part
        row = pl.multiple_of(s * LANES, LANES)
        spot = 0
        for j in range(4):
            rows = slice(j * LANES, (j + 1) * LANES)
            for k in range(j):
                diag[part, rows, k * LANES : (k + 1) * LANES] = off[
                    pl.ds(pl.multiple_of(spot * block + row, LANES), LANES), :
                ]
                spot += 1
            pair = pl.multiple_of(step * LANES, LANES)
            both = tail[j, pl.ds(pair, LANES), :].astype(jnp.float32)
            if part == 0:
                mine = jnp.where(down >= across, both, 0.0)
            else:
                pivots = tail[j, tri : tri + SPARE, :].astype(jnp.float32)
                which = lax.broadcasted_iota(jnp.int32, (SPARE, LANES), 0) == step
                pivot = jnp.sum(jnp.where(which, pivots, 0.0), axis=0, keepdims=True)
                mine = jnp.where(
                    down > across, both.T, jnp.where(down == across, pivot, 0.0)
                )
            diag[part, rows, rows] = mine.astype(diag.dtype)
            if j % 2 == 0:
                diag[part, rows, (j + 1) * LANES : (j + 2) * LANES] = zero
            first = tri + SPARE + s * below_rows * (below_width // LANES)
            for k in range(below_width // LANES):
                below[j * below_rows : (j + 1) * below_rows, k * LANES : (k + 1) * LANES] = tail[
                    j, pl.ds(pl.multiple_of(first + k * below_rows, 16), below_rows), :
                ]
        half = 2 * LANES
        x = source_ref[part]
        solved_ref[0, part, :, :half] = dot_rows(
            x[:, :half], diag[part, :half, :half]
        ).astype(solved_ref.dtype)
        solved_ref[0, part, :, half:] = dot_rows(x, diag[part, half:, :]).astype(solved_ref.dtype)
        update_ref[part] = dot_rows(solved_ref[0, part], below[...]).astype(update_ref.dtype)


def solve(place, source, first_block, height, sizes, own, lefts, rights, group_at, prior):
    tiers, per_device, below_rows = sizes
    _, columns, width = source.shape
    below = 4 * below_rows
    block, _, _, total = layout(per_device, below_rows, width)
    has_prior = prior is not None
    operands = [place, source, *own, *lefts, *rights] + ([prior] if has_prior else [])
    return pl.pallas_call(
        functools.partial(solve_kernel, group_at, has_prior),
        grid=(per_device // 2,),
        in_specs=[SMEM, pl.BlockSpec((2, columns, width), lambda i: (first_block + i, 0, 0))]
        + [ANY] * (len(operands) - 2),
        out_specs=[
            pl.BlockSpec((1, 2, columns, width), lambda i: (height, i, 0, 0)),
            pl.BlockSpec((2, columns, below), lambda i: (i, 0, 0)),
        ],
        out_shape=[
            jax.ShapeDtypeStruct((tiers, per_device, columns, width), jnp.bfloat16),
            jax.ShapeDtypeStruct((per_device, columns, below), jnp.bfloat16),
        ],
        scratch_shapes=[
            pltpu.VMEM((4, total - block, LANES), jnp.bfloat16),
            pltpu.VMEM((6 * block, LANES), jnp.bfloat16),
            pltpu.VMEM((2, width, width), jnp.bfloat16),
            pltpu.VMEM((below, width), jnp.bfloat16),
            pltpu.SemaphoreType.DMA((8,)),
        ],
        input_output_aliases={len(operands) - 1: 0} if has_prior else {},
        compiler_params=pltpu.CompilerParams(vmem_limit_bytes=32 << 20),
        cost_estimate=pl.CostEstimate(
            flops=2 * per_device * columns * width * (width + below),
            bytes_accessed=6 * per_device * columns * width,
            transcendentals=0,
        ),
        name=f"solve_{height}",
    )(*operands)


def after(value, *earlier):
    return lax.optimization_barrier((value, *(e.reshape(-1, LANES)[:8] for e in earlier)))[0]


def send(value, route):
    return lax.ppermute(value, "col", route)


def line_plan(histograms, diag_inv, below_panel, parent_map, row_lists):
    tiers, per_device, columns, width = histograms.shape
    below_rows = below_panel.shape[2]
    block, _, _, total = layout(per_device, below_rows, width)
    place = lax.axis_index("col").astype(jnp.int32)
    place_ref = place[None]
    up = [(0, 1), (1, 2), (2, 3)]
    down = [(1, 0), (2, 1), (3, 2)]
    packs = []
    for t in range(tiers):
        panels = below_panel
        if t > 0:
            panels = lax.optimization_barrier((below_panel, packs[t - 1][0]))[0]
        packs.append(pack(place_ref, diag_inv, panels, t))

    pairs = [(0, 1), (1, 0), (2, 3), (3, 2)]
    middle = [(1, 2), (2, 1)]
    lefts, rights = [], []
    if PLAN == "SM":
        for t, (base, rest) in enumerate(packs):
            if TIE and t >= TIE:
                ref = lefts[t - TIE] + rights[t - TIE][0]
                base = after(base, *[ref[i] for i in TIE_TO])
            s0 = send(base, pairs)
            m0 = send(base, middle)
            s1 = send(jnp.where(place == 3, rest, m0), pairs)
            second = jnp.where(place == 2, rest[block : 2 * block], s0[:block])
            m1 = send(jnp.concatenate([second, s0[block:]], 0), middle)
            m2 = send(s1[: 3 * block], middle[1:])
            second = jnp.where(place == 2, rest[block : 2 * block], m1[:block])
            s2 = send(jnp.concatenate([second, m1[block:]], 0), [(1, 0), (2, 3)])
            s3 = send(m2, [(1, 0)])
            lefts.append((s0, s1, s2, s3))
            rights.append(((m0, m1, m2), 0))
    else:
        for t, (base, rest) in enumerate(packs):
            if TIE and t >= TIE:
                base = after(base, *[lefts[t - TIE][i] for i in TIE_TO])
            left0 = send(base, down)
            mixed = jnp.concatenate([rest[block : 2 * block], left0[block:]], 0)
            left1 = send(jnp.where(place == 1, left0, jnp.where(place == 2, mixed, rest)), down)
            left2 = send(left1, down[:2])
            left3 = send(left2[: 3 * block], down[:1])
            lefts.append((left0, left1, left2, left3))
        for group in RIGHT_GROUPS:
            bases = jnp.stack([packs[t][0] for t in group])
            if group[0] > 0:
                bases = after(bases, lefts[group[0] - 1][1])
            right0 = send(bases, up)
            right1 = send(right0, up[1:])
            second = jnp.stack([packs[t][1][block : 2 * block] for t in group])
            right2 = send(jnp.concatenate([second, right1[:, block:]], 1), up[2:])
            rights += [((right0, right1, right2), i) for i in range(len(group))]

    myself = lax.axis_index("leaf")
    count = lax.axis_size("leaf")
    bit_count = max(count.bit_length() - 1, 1)
    table = jnp.concatenate([parent_map[:, :, None], row_lists], 2)
    tables = []
    for t in range(tiers - 1):
        mine = after(table[t], lefts[0][0]) if TABLE_TIE else table[t]
        tables.append(lax.ppermute(mine, "leaf", swap_route("leaf", t % bit_count)))
    source, first_block = histograms.reshape(-1, columns, width), 0
    solved = None
    for t in range(tiers):
        right, group_at = rights[t]
        solved, update = solve(
            place_ref,
            source,
            first_block,
            t,
            (tiers, per_device, below_rows),
            packs[t],
            lefts[t],
            right,
            group_at,
            solved,
        )
        if t == tiers - 1:
            break
        bit = t % bit_count
        peer = lax.ppermute(update, "leaf", swap_route("leaf", bit))
        partner = jnp.bitwise_xor(myself, 1 << bit)
        theirs = tables[t]
        parents = jnp.concatenate([parent_map[t], theirs[:, 0]])
        exists = jnp.repeat(jnp.stack([partner >= 0, partner < count]), per_device)
        mine = jnp.logical_and(parents // per_device == myself, exists)
        slots = jnp.where(mine, parents % per_device, -1)
        source = source_of(histograms, t + 1, update, peer, slots, row_lists[t], theirs[:, 1:])
        first_block = 0
    return solved, update


def on_device(histograms, diag_inv, below_panel, parent_map, row_lists):
    _, per_device, rows, width = diag_inv.shape
    fits = (
        lax.axis_size("col") == 4
        and rows == LANES
        and width == 4 * rows
        and per_device % 2 == 0
        and per_device <= 2 * SPARE
        and below_panel.shape[2] % 16 == 0
        and histograms.shape[2] % 16 == 0
        and histograms.shape[0] > 1
    )
    plan = line_plan if fits else gathered_plan
    return plan(histograms, diag_inv, below_panel, parent_map, row_lists)


def solution(mesh):
    return jax.shard_map(
        on_device,
        mesh=mesh,
        in_specs=(
            P(None, "leaf", "col", None),
            P(None, "leaf", "col", None),
            P(None, "leaf", "col", None),
            P(None, "leaf"),
            P(None, "leaf", None),
        ),
        out_specs=(P(None, "leaf", "col", None), P("leaf", "col", None)),
        check_vma=False,
    )
```

```python
import functools

import jax
import jax.numpy as jnp
from jax import lax
from jax.experimental import pallas as pl
from jax.experimental.pallas import tpu as pltpu
from jax.sharding import PartitionSpec as P

TIE = 0
TIE_TO = (1,)
TABLE_TIE = True
RIGHT_GROUPS = [[0], [1], [2], [3]]
LANES = 128
SPARE = 16
ANY = pl.BlockSpec(memory_space=pl.ANY)
SMEM = pl.BlockSpec(memory_space=pltpu.SMEM)


def swap_route(axis, apart):
    count = lax.axis_size(axis)
    pairs = []
    for low in range(count):
        high = low | 1 << apart
        if high != low and high < count:
            pairs += [(low, high), (high, low)]
    return pairs


def dot_rows(left, right):
    return lax.dot_general(
        left, right, (((1,), (1,)), ((), ())), preferred_element_type=jnp.float32
    )


def spread_rows(update, lists, slots, per_device, node_width):
    slot_match = (
        slots[:, None, None, None] == jnp.arange(per_device, dtype=jnp.int32)[None, None, :, None]
    )
    row_match = (
        lists[:, :, None, None] == jnp.arange(node_width, dtype=jnp.int32)[None, None, None, :]
    )
    placing = jnp.logical_and(slot_match, row_match).astype(jnp.bfloat16)
    return jnp.einsum(
        "scr,srpw->pcw", update.astype(jnp.bfloat16), placing, preferred_element_type=jnp.float32
    )


def gathered_plan(histograms, diag_inv, below_panel, parent_map, row_lists):
    tier_count, per_device, _, node_width = histograms.shape
    bit_count = max(lax.axis_size("leaf").bit_length() - 1, 1)
    myself = lax.axis_index("leaf")
    incoming = jnp.zeros(histograms.shape[1:], jnp.float32)
    solved = []
    for height in range(tier_count):
        source = (histograms[height].astype(jnp.float32) - incoming).astype(jnp.bfloat16)
        diag = lax.all_gather(diag_inv[height], "col", axis=1, tiled=True)
        below = lax.all_gather(below_panel[height], "col", axis=1, tiled=True)
        answer = jnp.einsum(
            "scw,svw->scv", source, diag, preferred_element_type=jnp.float32
        ).astype(jnp.bfloat16)
        solved.append(answer)
        update = jnp.einsum("scw,srw->scr", answer, below, preferred_element_type=jnp.float32)
        if height == tier_count - 1:
            break
        owners = parent_map[height] // per_device
        slots = parent_map[height] % per_device
        staying = owners == myself
        lists = row_lists[height]
        kept = spread_rows(update, lists, jnp.where(staying, slots, -1), per_device, node_width)
        leaving = spread_rows(update, lists, jnp.where(staying, -1, slots), per_device, node_width)
        path = swap_route("leaf", height % bit_count)
        arrived = lax.ppermute(leaving.astype(jnp.bfloat16), "leaf", path)
        incoming = kept + arrived.astype(jnp.float32)
    return jnp.stack(solved), update.astype(jnp.bfloat16)


def layout(per_device, below_rows, node_width):
    block = per_device * LANES
    tri = block // 2
    below = per_device * below_rows * (node_width // LANES)
    return block, tri, below, block + tri + SPARE + below


def pack_kernel(place_ref, diag_ref, below_ref, base_ref, rest_ref):
    per_device, below_rows, node_width = below_ref.shape[1:]
    block, tri, _, total = layout(per_device, below_rows, node_width)
    for s in range(per_device):
        rows = slice(s * LANES, (s + 1) * LANES)
        base_ref[rows, :] = diag_ref[0, s, :, :LANES]
        for k in range(3):
            rest_ref[k * block + s * LANES : k * block + (s + 1) * LANES, :] = diag_ref[
                0, s, :, k * LANES : (k + 1) * LANES
            ]
        start = block + tri + SPARE + s * below_rows * (node_width // LANES)
        for k in range(node_width // LANES):
            base_ref[start + k * below_rows : start + (k + 1) * below_rows, :] = below_ref[
                0, s, :, k * LANES : (k + 1) * LANES
            ]
    rest_ref[3 * block :, :] = jnp.zeros((total - 3 * block, LANES), rest_ref.dtype)
    down = lax.broadcasted_iota(jnp.int32, (LANES, LANES), 0)
    across = lax.broadcasted_iota(jnp.int32, (LANES, LANES), 1)
    for place in range(4):

        @pl.when(place_ref[0] == place)
        def _():
            columns = slice(place * LANES, (place + 1) * LANES)
            pivots = []
            for pair in range(per_device // 2):
                first = diag_ref[0, 2 * pair, :, columns].astype(jnp.float32)
                second = diag_ref[0, 2 * pair + 1, :, columns].astype(jnp.float32)
                both = jnp.where(down >= across, first, second.T)
                base_ref[block + pair * LANES : block + (pair + 1) * LANES, :] = both.astype(
                    base_ref.dtype
                )
                pivots.append(
                    jnp.sum(jnp.where(down == across, second, 0.0), axis=0, keepdims=True)
                )
            pivots.append(jnp.zeros((SPARE - len(pivots), LANES), jnp.float32))
            base_ref[block + tri : block + tri + SPARE, :] = jnp.concatenate(pivots, 0).astype(
                base_ref.dtype
            )


def pack(place, diag_inv, below_panel, height):
    _, per_device, rows, node_width = diag_inv.shape
    below_rows = below_panel.shape[2]
    total = layout(per_device, below_rows, node_width)[-1]
    shape = jax.ShapeDtypeStruct((total, LANES), diag_inv.dtype)
    return pl.pallas_call(
        pack_kernel,
        grid=(1,),
        in_specs=[
            SMEM,
            pl.BlockSpec((1, per_device, rows, node_width), lambda i: (height, 0, 0, 0)),
            pl.BlockSpec((1, per_device, below_rows, node_width), lambda i: (height, 0, 0, 0)),
        ],
        out_specs=[pl.BlockSpec((total, LANES), lambda i: (0, 0))] * 2,
        out_shape=[shape, shape],
        cost_estimate=pl.CostEstimate(
            flops=0, bytes_accessed=4 * total * LANES * 2, transcendentals=0
        ),
        name=f"pack_{height}",
    )(place, diag_inv, below_panel)


def source_kernel(slots_ref, hist_ref, own_ref, peer_ref, own_lists, peer_lists, out_ref, total):
    per_device, below = own_ref.shape[0], own_ref.shape[2]
    width = out_ref.shape[2]
    total[...] = hist_ref[0].astype(jnp.float32)
    target = lax.broadcasted_iota(jnp.int32, (width, below), 0)
    for refs in ((own_ref, own_lists, 0), (peer_ref, peer_lists, per_device)):
        update_ref, lists_ref, offset = refs
        for s in range(per_device):
            slot = slots_ref[offset + s]

            @pl.when(slot >= 0)
            def _():
                here = target == lists_ref[s : s + 1, :]
                placing = jnp.where(here, 1.0, 0.0).astype(jnp.bfloat16)
                total[slot] = total[slot] - dot_rows(update_ref[s], placing)

    out_ref[...] = total[...].astype(out_ref.dtype)


def source_of(histograms, height, own, peer, slots, own_lists, peer_lists):
    _, per_device, columns, width = histograms.shape
    below = own.shape[2]
    whole = pl.BlockSpec((per_device, columns, below), lambda i: (0, 0, 0))
    lists = pl.BlockSpec((per_device, below), lambda i: (0, 0))
    return pl.pallas_call(
        source_kernel,
        grid=(1,),
        in_specs=[
            SMEM,
            pl.BlockSpec((1, per_device, columns, width), lambda i: (height, 0, 0, 0)),
            whole,
            whole,
            lists,
            lists,
        ],
        out_specs=pl.BlockSpec((per_device, columns, width), lambda i: (0, 0, 0)),
        out_shape=jax.ShapeDtypeStruct((per_device, columns, width), jnp.bfloat16),
        scratch_shapes=[pltpu.VMEM((per_device, columns, width), jnp.float32)],
        compiler_params=pltpu.CompilerParams(vmem_limit_bytes=32 << 20),
        cost_estimate=pl.CostEstimate(
            flops=4 * per_device * columns * width * below,
            bytes_accessed=6 * per_device * columns * width,
            transcendentals=0,
        ),
        name=f"source_{height}",
    )(slots, histograms, own, peer, own_lists, peer_lists)


def solve_kernel(
    group_at,
    has_prior,
    place_ref,
    source_ref,
    base,
    rest,
    left0,
    left1,
    left2,
    left3,
    right0,
    right1,
    right2,
    *refs,
):
    if has_prior:
        refs = refs[1:]
    solved_ref, update_ref, tail, off, diag, below, sems = refs
    below_width = below.shape[1]
    below_rows = below.shape[0] // 4
    block = off.shape[0] // 6
    tri = block // 2
    step = pl.program_id(0)

    @pl.when(step == 0)
    def _():
        def head(ref):
            return ref.at[pl.ds(0, block)]

        def foot(ref):
            return ref.at[pl.ds(block, tail.shape[1])]

        def all_off(ref):
            return ref.at[pl.ds(0, 3 * block)]

        r0, r1, r2 = (r.at[group_at] for r in (right0, right1, right2))
        second = rest.at[pl.ds(block, block)]
        where = (
            (foot(base), foot(left0), foot(left1), foot(left2),
             head(left0), head(left1), head(left2), all_off(left3)),
            (foot(r0), foot(base), foot(left0), foot(left1),
             head(base), head(left0), head(left1), all_off(left2)),
            (foot(r1), foot(r0), foot(base), foot(left0),
             head(r0), head(base), second, all_off(left1)),
            (foot(r2), foot(r1), foot(r0), foot(base),
             head(r1), head(r0), head(r2), all_off(rest)),
        )
        into = [tail.at[j] for j in range(4)]
        into += [off.at[pl.ds(k * block, block)] for k in range(3)]
        into += [off.at[pl.ds(3 * block, 3 * block)]]
        for place in range(4):

            @pl.when(place_ref[0] == place)
            def _():
                copies = [
                    pltpu.make_async_copy(src, dst, sems.at[i])
                    for i, (src, dst) in enumerate(zip(where[place], into))
                ]
                for copy in copies:
                    copy.start()
                for copy in copies:
                    copy.wait()

    down = lax.broadcasted_iota(jnp.int32, (LANES, LANES), 0)
    across = lax.broadcasted_iota(jnp.int32, (LANES, LANES), 1)
    zero = jnp.zeros((LANES, LANES), diag.dtype)
    per_step = solved_ref.shape[1]
    for part in range(per_step):
        s = step * per_step + part
        row = pl.multiple_of(s * LANES, LANES)
        spot = 0
        for j in range(4):
            rows = slice(j * LANES, (j + 1) * LANES)
            for k in range(j):
                diag[part, rows, k * LANES : (k + 1) * LANES] = off[
                    pl.ds(pl.multiple_of(spot * block + row, LANES), LANES), :
                ]
                spot += 1
            pair = pl.multiple_of(step * LANES, LANES)
            both = tail[j, pl.ds(pair, LANES), :].astype(jnp.float32)
            if part == 0:
                mine = jnp.where(down >= across, both, 0.0)
            else:
                pivots = tail[j, tri : tri + SPARE, :].astype(jnp.float32)
                which = lax.broadcasted_iota(jnp.int32, (SPARE, LANES), 0) == step
                pivot = jnp.sum(jnp.where(which, pivots, 0.0), axis=0, keepdims=True)
                mine = jnp.where(
                    down > across, both.T, jnp.where(down == across, pivot, 0.0)
                )
            diag[part, rows, rows] = mine.astype(diag.dtype)
            if j % 2 == 0:
                diag[part, rows, (j + 1) * LANES : (j + 2) * LANES] = zero
            first = tri + SPARE + s * below_rows * (below_width // LANES)
            for k in range(below_width // LANES):
                below[j * below_rows : (j + 1) * below_rows, k * LANES : (k + 1) * LANES] = tail[
                    j, pl.ds(pl.multiple_of(first + k * below_rows, 16), below_rows), :
                ]
        half = 2 * LANES
        x = source_ref[part]
        solved_ref[0, part, :, :half] = dot_rows(
            x[:, :half], diag[part, :half, :half]
        ).astype(solved_ref.dtype)
        solved_ref[0, part, :, half:] = dot_rows(x, diag[part, half:, :]).astype(solved_ref.dtype)
        update_ref[part] = dot_rows(solved_ref[0, part], below[...]).astype(update_ref.dtype)


def solve(place, source, first_block, height, sizes, own, lefts, rights, group_at, prior):
    tiers, per_device, below_rows = sizes
    _, columns, width = source.shape
    below = 4 * below_rows
    block, _, _, total = layout(per_device, below_rows, width)
    has_prior = prior is not None
    operands = [place, source, *own, *lefts, *rights] + ([prior] if has_prior else [])
    return pl.pallas_call(
        functools.partial(solve_kernel, group_at, has_prior),
        grid=(per_device // 2,),
        in_specs=[SMEM, pl.BlockSpec((2, columns, width), lambda i: (first_block + i, 0, 0))]
        + [ANY] * (len(operands) - 2),
        out_specs=[
            pl.BlockSpec((1, 2, columns, width), lambda i: (height, i, 0, 0)),
            pl.BlockSpec((2, columns, below), lambda i: (i, 0, 0)),
        ],
        out_shape=[
            jax.ShapeDtypeStruct((tiers, per_device, columns, width), jnp.bfloat16),
            jax.ShapeDtypeStruct((per_device, columns, below), jnp.bfloat16),
        ],
        scratch_shapes=[
            pltpu.VMEM((4, total - block, LANES), jnp.bfloat16),
            pltpu.VMEM((6 * block, LANES), jnp.bfloat16),
            pltpu.VMEM((2, width, width), jnp.bfloat16),
            pltpu.VMEM((below, width), jnp.bfloat16),
            pltpu.SemaphoreType.DMA((8,)),
        ],
        input_output_aliases={len(operands) - 1: 0} if has_prior else {},
        compiler_params=pltpu.CompilerParams(vmem_limit_bytes=32 << 20),
        cost_estimate=pl.CostEstimate(
            flops=2 * per_device * columns * width * (width + below),
            bytes_accessed=6 * per_device * columns * width,
            transcendentals=0,
        ),
        name=f"solve_{height}",
    )(*operands)


def after(value, *earlier):
    return lax.optimization_barrier((value, *(e.reshape(-1, LANES)[:8] for e in earlier)))[0]


def send(value, route):
    return lax.ppermute(value, "col", route)


def line_plan(histograms, diag_inv, below_panel, parent_map, row_lists):
    tiers, per_device, columns, width = histograms.shape
    below_rows = below_panel.shape[2]
    block, _, _, total = layout(per_device, below_rows, width)
    place = lax.axis_index("col").astype(jnp.int32)
    place_ref = place[None]
    up = [(0, 1), (1, 2), (2, 3)]
    down = [(1, 0), (2, 1), (3, 2)]
    packs = []
    for t in range(tiers):
        panels = below_panel
        if t > 0:
            panels = lax.optimization_barrier((below_panel, packs[t - 1][0]))[0]
        packs.append(pack(place_ref, diag_inv, panels, t))

    lefts, rights = [], []
    for t, (base, rest) in enumerate(packs):
        if TIE and t >= TIE:
            base = after(base, *[lefts[t - TIE][i] for i in TIE_TO])
        left0 = send(base, down)
        mixed = jnp.concatenate([rest[block : 2 * block], left0[block:]], 0)
        left1 = send(jnp.where(place == 1, left0, jnp.where(place == 2, mixed, rest)), down)
        left2 = send(left1, down[:2])
        straight = t == tiers - 1
        left3 = send(rest[: 3 * block], [(3, 0)]) if straight else send(left2[: 3 * block], down[:1])
        lefts.append((left0, left1, left2, left3))
    for group in RIGHT_GROUPS:
        bases = jnp.stack([packs[t][0] for t in group])
        if group[0] > 0:
            bases = after(bases, lefts[group[0] - 1][1])
        right0 = send(bases, up)
        right1 = send(right0, up[1:])
        second = jnp.stack([packs[t][1][block : 2 * block] for t in group])
        right2 = send(jnp.concatenate([second, right1[:, block:]], 1), up[2:])
        rights += [((right0, right1, right2), i) for i in range(len(group))]

    myself = lax.axis_index("leaf")
    count = lax.axis_size("leaf")
    bit_count = max(count.bit_length() - 1, 1)
    table = jnp.concatenate([parent_map[:, :, None], row_lists], 2)
    tables = []
    for t in range(tiers - 1):
        mine = after(table[t], lefts[0][0]) if TABLE_TIE else table[t]
        tables.append(lax.ppermute(mine, "leaf", swap_route("leaf", t % bit_count)))
    source, first_block = histograms.reshape(-1, columns, width), 0
    solved = None
    for t in range(tiers):
        right, group_at = rights[t]
        solved, update = solve(
            place_ref,
            source,
            first_block,
            t,
            (tiers, per_device, below_rows),
            packs[t],
            lefts[t],
            right,
            group_at,
            solved,
        )
        if t == tiers - 1:
            break
        bit = t % bit_count
        peer = lax.ppermute(update, "leaf", swap_route("leaf", bit))
        partner = jnp.bitwise_xor(myself, 1 << bit)
        theirs = tables[t]
        parents = jnp.concatenate([parent_map[t], theirs[:, 0]])
        exists = jnp.repeat(jnp.stack([partner >= 0, partner < count]), per_device)
        mine = jnp.logical_and(parents // per_device == myself, exists)
        slots = jnp.where(mine, parents % per_device, -1)
        source = source_of(histograms, t + 1, update, peer, slots, row_lists[t], theirs[:, 1:])
        first_block = 0
    return solved, update


def on_device(histograms, diag_inv, below_panel, parent_map, row_lists):
    _, per_device, rows, width = diag_inv.shape
    fits = (
        lax.axis_size("col") == 4
        and rows == LANES
        and width == 4 * rows
        and per_device % 2 == 0
        and per_device <= 2 * SPARE
        and below_panel.shape[2] % 16 == 0
        and histograms.shape[2] % 16 == 0
        and histograms.shape[0] > 1
    )
    plan = line_plan if fits else gathered_plan
    return plan(histograms, diag_inv, below_panel, parent_map, row_lists)


def solution(mesh):
    return jax.shard_map(
        on_device,
        mesh=mesh,
        in_specs=(
            P(None, "leaf", "col", None),
            P(None, "leaf", "col", None),
            P(None, "leaf", "col", None),
            P(None, "leaf"),
            P(None, "leaf", None),
        ),
        out_specs=(P(None, "leaf", "col", None), P("leaf", "col", None)),
        check_vma=False,
    )
```
